32 devices in a mesh: groups: 2 (over x), tile: 16 (over z, y, core).
Axes of the slice: x: 2, y: 2, z: 4, core: 2. Of those that a mesh axis runs over, the one named last changes fastest.
Arguments:
- tile_values: bfloat16 [320, 512, 512], P(('groups', 'tile')), parts along dimension 0, may hold values from 0.05 to 5
- tile_rows: int32 [320], P(('groups', 'tile')), parts along dimension 0, may hold values from 0 to 15, as said below
- tile_cols: int32 [320], P(('groups', 'tile')), parts along dimension 0, may hold values from 0 to 15
- tile_live: int32 [320], P(('groups', 'tile')), parts along dimension 0, may hold values from 0 to 1, as said below
- bias: float32 [32, 512], P(('groups', 'tile')), parts along dimension 0, may hold values from 0.5 to 2
Outputs:
- balanced: float32 [32, 512], P(('groups', 'tile')), parts along dimension 0
- coverage: float32 [32, 512], P(('groups', 'tile')), parts along dimension 0
The draws below stay inside these ranges and needn't reach their ends.
There are 2 independent parts, one for each index of `groups`. The reference program is written for one: setup_inputs(seed, part) draws one part's arguments, and reference() takes and returns one part's arrays. A program takes and returns all parts, laid end to end along the dimension named above; each array names one. Nothing has to cross between parts.
Inputs may be any that keep to these rules, and one draw needn't show every extreme that they name: `tile_live`: within each device's 10 slots the live ones come first. Device d holds the band tiles of its own 1 bin blocks (row block owned, column block minus row block 0 to 7, within the map), then 0 to 2 trans tiles; every bin block has its diagonal tile; some device has all 10 slots live. On live slots tile_rows <= tile_cols; trans tiles lie anywhere.
All inputs are finite; a program needn't handle non-finite values.
Results may differ from the reference program's by a relative error of at most 0.00035.
Values sent between devices are 32-bit elements; how exact they have to be, the bound alone decides.
A program may use at most 64 MiB of HBM per device.

```python
import math
import jax
import jax.numpy as jnp
from jax import lax

TS = 512
BAND = 8
ITERS = 2
BLK_DEV = 1
TPD = 10
NBLK = 16
SLOTS = 160


def layout(key):
    devices = SLOTS // TPD
    subkeys = jax.random.split(key, 5)
    band_slots = BLK_DEV * BAND
    spare = TPD - band_slots
    device_ids = jnp.arange(devices)[:, None]
    position = jnp.arange(TPD)[None, :]
    owned = device_ids * BLK_DEV + jnp.minimum(position // BAND, BLK_DEV - 1)
    band_col = owned + position % BAND
    in_band = position < band_slots
    band_live = in_band & (band_col < NBLK)
    extra_count = jnp.minimum(jax.random.randint(subkeys[0], (devices,), 0, spare + 1), jax.random.randint(subkeys[1], (devices,), 0, spare + 1))
    fullest = jax.random.randint(subkeys[2], (), 0, devices - BAND)
    extra_count = jnp.where(jnp.arange(devices) == fullest, spare, extra_count)
    trans_live = (position >= band_slots) & (position - band_slots < extra_count[:, None])
    anchor = jax.random.randint(subkeys[3], (devices, TPD), 0, NBLK)
    partner = jax.random.randint(subkeys[4], (devices, TPD), 0, NBLK)
    rows_raw = jnp.where(in_band, owned, jnp.minimum(anchor, partner))
    cols_raw = jnp.where(in_band, jnp.minimum(band_col, NBLK - 1), jnp.maximum(anchor, partner))
    live_raw = (band_live | trans_live).astype(jnp.int32)
    order_key = jnp.where(live_raw == 1, position, position + TPD) + jnp.zeros((devices, TPD), jnp.int32)
    order = jnp.argsort(order_key, axis=1, stable=True)
    tile_rows = jnp.take_along_axis(rows_raw, order, axis=1).astype(jnp.int32)
    tile_cols = jnp.take_along_axis(cols_raw, order, axis=1).astype(jnp.int32)
    tile_live = jnp.take_along_axis(live_raw, order, axis=1).astype(jnp.int32)
    return (tile_rows.reshape(-1), tile_cols.reshape(-1), tile_live.reshape(-1))


def draw_tile_rows(key, part):
    return layout(key)[0]


def draw_tile_cols(key, part):
    return layout(key)[1]


def draw_tile_live(key, part):
    return layout(key)[2]


def draw_tile_values(key, part):
    tile_rows, tile_cols, tile_live = layout(key)
    key = jax.random.fold_in(key, 11)
    subkeys = jax.random.split(key, 3)
    period = TS / 4.0
    decay_len = TS / 8.0
    offsets = jnp.arange(TS).astype(jnp.float32)
    bins = jnp.arange(NBLK * TS).astype(jnp.float32).reshape(NBLK, TS)
    phase = jax.random.uniform(subkeys[0], (), jnp.float32, 0.0, 2.0 * math.pi)
    smooth = 0.7 + 0.3 * jnp.sin(2.0 * math.pi * bins / period + phase)
    rough = jnp.exp(jax.random.uniform(subkeys[1], (NBLK, TS), jnp.float32, math.log(0.5), 0.0))
    level = jnp.exp(jax.random.uniform(subkeys[2], (SLOTS, TS, TS), jnp.float32, math.log(0.2), 0.0))
    visible = rough * smooth
    row_vis = jnp.take(visible, tile_rows, axis=0)
    col_vis = jnp.take(visible, tile_cols, axis=0)
    row_pos = tile_rows.astype(jnp.float32)[:, None] * TS + offsets[None, :]
    col_pos = tile_cols.astype(jnp.float32)[:, None] * TS + offsets[None, :]
    distance = jnp.abs(row_pos[:, :, None] - col_pos[:, None, :])
    decay = (1.0 / (1.0 + distance / decay_len) + 0.2) / 1.2
    values = 8.0 * level * row_vis[:, :, None] * col_vis[:, None, :] * decay
    return jnp.clip(values, 0.05, 5.0).astype(jnp.bfloat16)


def steps_of(own_key, extent, cuts, least, high):
    level = 1.0
    for dim, parts in cuts:
        draws = jax.random.uniform(jax.random.fold_in(jax.random.fold_in(own_key, 6), dim), (parts,), jnp.float32, least / len(cuts), high / len(cuts))
        level = level * jnp.repeat(jnp.exp(draws), extent[dim] // parts).reshape((-1,) + (1,) * (len(extent) - 1 - dim))
    return level


def setup_inputs(seed: int = 0, part: int = 0) -> dict:
    key_list = jax.random.split(jax.random.key(seed), 6)
    part_splits = jax.random.split(jax.random.fold_in(key_list[5], part), 6)
    return {
        "tile_values": draw_tile_values(jax.random.fold_in(jax.random.fold_in(key_list[5], part), 71), part),
        "tile_rows": draw_tile_rows(jax.random.fold_in(jax.random.fold_in(key_list[5], part), 71), part),
        "tile_cols": draw_tile_cols(jax.random.fold_in(jax.random.fold_in(key_list[5], part), 71), part),
        "tile_live": draw_tile_live(jax.random.fold_in(jax.random.fold_in(key_list[5], part), 71), part),
        "bias": jnp.clip(jnp.exp(math.log(2.0) - 1.3862944 * jax.random.uniform(part_splits[4], (NBLK, TS), jnp.float32) ** steps_of(part_splits[4], (NBLK, TS), ((0, 16),), -0.2, 0.2)), 0.5, 2.0),
    }


def tile_margins(tile_values, tile_rows, tile_cols, tile_live, scales):
    def add_tile(totals, slot_entry):
        values, row_block, col_block, live_flag = slot_entry
        weight = jnp.where(row_block == col_block, 0.5, 1.0).astype(jnp.float32) * live_flag.astype(jnp.float32)
        matrix = values.astype(jnp.float32)
        row_scales = lax.dynamic_index_in_dim(scales, row_block, 0, keepdims=False)
        col_scales = lax.dynamic_index_in_dim(scales, col_block, 0, keepdims=False)
        to_rows = jnp.dot(matrix, col_scales, precision=lax.Precision.HIGHEST) * weight
        to_cols = jnp.dot(row_scales, matrix, precision=lax.Precision.HIGHEST) * weight
        totals = totals.at[row_block].add(to_rows)
        totals = totals.at[col_block].add(to_cols)
        return totals, None

    start = jnp.zeros((NBLK, TS), jnp.float32)
    totals, _ = lax.scan(add_tile, start, (tile_values, tile_rows, tile_cols, tile_live))
    return scales * totals


def reference(tile_values, tile_rows, tile_cols, tile_live, bias):
    scales = bias
    coverage = bias
    for sweep in range(ITERS):
        margin = tile_margins(tile_values, tile_rows, tile_cols, tile_live, scales)
        average = jnp.mean(margin)
        coverage = margin / average
        scales = scales / coverage
    return scales, coverage
```

```python
import functools

import jax
import jax.numpy as jnp
from jax import lax
from jax.experimental import pallas as pl
from jax.experimental.pallas import tpu as pltpu
from jax.sharding import PartitionSpec as P

ITERS = 2
BAND = 8
TRANS = 2
LANES = 128
MESH = pl.DeviceIdType.MESH


def each_peer(me, n, body):
    if n <= 16:
        for step in range(1, n):
            body(lax.rem(me + step, n))
    else:

        @pl.loop(1, n)
        def _(step):
            body(lax.rem(me + step, n))


def kernel(
    n, values, rows_in, cols_in, live_in, bias_in, balanced, coverage,
    tiles, rows, cols, live, bias, scales0, scales1, send0, send1, recv0, recv1,
    tile_sem, small_sem, out_sem, in_sem,
):
    group = lax.axis_index("groups")
    me = lax.axis_index("tile")
    slots, width = values.shape[0], values.shape[1]
    parts = width // LANES
    messages = parts + 1

    smalls = [
        pltpu.make_async_copy(source, target, small_sem.at[index])
        for index, (source, target) in enumerate(
            ((bias_in, bias), (rows_in, rows), (cols_in, cols), (live_in, live))
        )
    ]
    loads = [
        pltpu.make_async_copy(values.at[slot], tiles.at[slot], tile_sem.at[slot])
        for slot in range(slots)
    ]
    for copy in smalls + loads:
        copy.start()

    barrier = pltpu.get_barrier_semaphore()
    each_peer(
        me,
        n,
        lambda peer: pl.semaphore_signal(
            barrier, inc=1, device_id=(group, peer), device_id_type=MESH
        ),
    )

    smalls[0].wait()
    for part in range(parts):
        scales0[me, part : part + 1, :] = bias[:, part * LANES : (part + 1) * LANES]
    pl.semaphore_wait(barrier, n - 1)

    def gather_start(scales, phase):
        each_peer(
            me,
            n,
            lambda peer: pltpu.make_async_remote_copy(
                src_ref=scales.at[me],
                dst_ref=scales.at[me],
                send_sem=out_sem.at[phase],
                recv_sem=in_sem.at[phase],
                device_id=(group, peer),
                device_id_type=MESH,
            ).start(),
        )

    def reduce_start(send, recv, phase):
        each_peer(
            me,
            n,
            lambda peer: pltpu.make_async_remote_copy(
                src_ref=send.at[peer],
                dst_ref=recv.at[me],
                send_sem=out_sem.at[phase],
                recv_sem=in_sem.at[phase],
                device_id=(group, peer),
                device_id_type=MESH,
            ).start(),
        )

    def arrived(buffer, sem):
        every = buffer.at[pl.ds(0, n - 1)]
        pltpu.make_async_copy(every, every, sem).wait()

    def as_row(buffer, index):
        return jnp.concatenate(
            [buffer[index, part : part + 1, :] for part in range(parts)], axis=1
        )

    def halves(vector):
        upper = vector.astype(jnp.bfloat16).astype(jnp.float32)
        return upper, vector - upper

    place = lax.broadcasted_iota(jnp.int32, (2 * n, width), 0)
    is_upper = place < n
    owner = jnp.where(is_upper, place, place - n)
    line = lax.broadcasted_iota(jnp.int32, (16, width), 0)

    def for_owner(vector, weight, target):
        upper, lower = halves(vector * weight)
        pair = jnp.where(is_upper, upper, lower)
        return jnp.where(owner == target, pair, 0.0).astype(jnp.bfloat16)

    def as_pair(vector, weight):
        upper, lower = halves(vector * weight)
        pair = jnp.where(line == 0, upper, jnp.where(line == 1, lower, 0.0))
        return pair.astype(jnp.bfloat16)

    def times(left, slot):
        return jnp.dot(left, tiles[slot], preferred_element_type=jnp.float32)

    def times_transposed(left, slot):
        return lax.dot_general(
            left, tiles[slot], (((1,), (1,)), ((), ())), preferred_element_type=jnp.float32
        )

    held = jnp.minimum(BAND, n - me)
    grands = []
    mine = None
    for sweep, (scales, send, recv) in enumerate(
        ((scales0, send0, recv0), (scales1, send1, recv1))
    ):
        gather_start(scales, 2 * sweep)
        if sweep == 0:
            for copy in smalls[1:]:
                copy.wait()
            mine = scales[me, 0:parts, :]
        band_cols = [cols[slot] for slot in range(BAND)]
        band_weights = [
            jnp.where(band_cols[slot] == me, 0.5, 1.0)
            * jnp.where(slot < held, 1.0, 0.0)
            for slot in range(BAND)
        ]
        own_row = as_row(scales, me)
        to_cols = jnp.zeros((2 * n, width), jnp.float32)
        for slot in range(BAND):
            if sweep == 0:
                loads[slot].wait()
            to_cols += times(for_owner(own_row, band_weights[slot], band_cols[slot]), slot)
        if sweep == 0:
            for copy in loads[BAND:]:
                copy.wait()

        arrived(scales, in_sem.at[2 * sweep])
        to_rows = jnp.zeros((n, width), jnp.float32)
        for extra in range(TRANS):
            slot = held + extra
            row, col = rows[slot], cols[slot]
            weight = jnp.where(row == col, 0.5, 1.0) * live[slot].astype(jnp.float32)
            to_cols += times(for_owner(as_row(scales, row), weight, col), slot)
            found = times_transposed(as_pair(as_row(scales, col), weight), slot)
            found = found[0:1] + found[1:2]
            to_rows += jnp.where(owner[:n] == row, found, 0.0)
        once = to_cols[:n] + to_cols[n:]
        both = once + to_rows
        flat_scales = scales.reshape(n * 8, LANES)
        flat_send = send.reshape(n * 8, LANES)
        form = jnp.zeros((n, LANES), jnp.float32)
        for part in range(parts):
            lanes = slice(part * LANES, (part + 1) * LANES)
            flat_send[pl.ds(part, n, stride=8), :] = both[:, lanes]
            form += once[:, lanes] * flat_scales[pl.ds(part, n, stride=8), :]
        form = jnp.sum(form, axis=0, keepdims=True)
        flat_send[pl.ds(parts, n, stride=8), :] = jnp.broadcast_to(form, (n, LANES))
        reduce_start(send, recv, 2 * sweep + 1)

        owned = jnp.zeros((16, width), jnp.float32)
        for slot in range(BAND):
            pair = as_pair(as_row(scales, band_cols[slot]), band_weights[slot])
            owned += times_transposed(pair, slot)
        owned = owned[0:1] + owned[1:2]
        owned += jnp.sum(jnp.where(owner[:n] == me, both, 0.0), axis=0, keepdims=True)
        for part in range(parts):
            recv[me, part : part + 1, :] = owned[:, part * LANES : (part + 1) * LANES]
        recv[me, parts:messages, :] = form
        arrived(recv, in_sem.at[2 * sweep + 1])
        total = jnp.sum(recv[:, 0:messages, :], axis=0)
        grands.append(2.0 * jnp.sum(total[parts:messages], keepdims=True))
        total = total[0:parts]
        if sweep + 1 < ITERS:
            mine = 1.0 / total
            scales1[me, 0:parts, :] = mine

    bins = float(n * width)
    over = mine * total * (bins / grands[1])
    result = mine * (grands[0] / bins) / over
    for part in range(parts):
        lanes = slice(part * LANES, (part + 1) * LANES)
        coverage[:, lanes] = over[part : part + 1]
        balanced[:, lanes] = result[part : part + 1]
    for phase, buffer in enumerate((scales0, send0, scales1, send1)):
        arrived(buffer, out_sem.at[phase])


def solution(mesh):
    n = mesh.shape["tile"]

    def shards(tile_values, tile_rows, tile_cols, tile_live, bias):
        slots, width = tile_values.shape[0], tile_values.shape[1]
        block = pltpu.VMEM((n, 8, LANES), jnp.float32)
        return pl.pallas_call(
            functools.partial(kernel, n),
            out_shape=(jax.ShapeDtypeStruct(bias.shape, jnp.float32),) * 2,
            in_specs=[pl.BlockSpec(memory_space=pltpu.HBM)] * 5,
            out_specs=(pl.BlockSpec(memory_space=pltpu.VMEM),) * 2,
            scratch_shapes=[
                pltpu.VMEM((slots, width, width), jnp.bfloat16),
                pltpu.SMEM((slots,), jnp.int32),
                pltpu.SMEM((slots,), jnp.int32),
                pltpu.SMEM((slots,), jnp.int32),
                pltpu.VMEM(bias.shape, jnp.float32),
                block, block, block, block, block, block,
                pltpu.SemaphoreType.DMA((slots,)),
                pltpu.SemaphoreType.DMA((4,)),
                pltpu.SemaphoreType.DMA((4,)),
                pltpu.SemaphoreType.DMA((4,)),
            ],
            compiler_params=pltpu.CompilerParams(
                collective_id=0, has_side_effects=True, vmem_limit_bytes=48 * 1024 * 1024
            ),
        )(tile_values, tile_rows, tile_cols, tile_live, bias)

    placed = (
        P(("groups", "tile"), None, None),
        P(("groups", "tile")),
        P(("groups", "tile")),
        P(("groups", "tile")),
        P(("groups", "tile"), None),
    )
    return jax.shard_map(
        shards,
        mesh=mesh,
        in_specs=placed,
        out_specs=(P(("groups", "tile"), None), P(("groups", "tile"), None)),
        check_vma=False,
    )
```

```python
import functools

import jax
import jax.numpy as jnp
from jax import lax
from jax.experimental import pallas as pl
from jax.experimental.pallas import tpu as pltpu
from jax.sharding import PartitionSpec as P

ITERS = 2
BAND = 8
TRANS = 2
LANES = 128
MESH = pl.DeviceIdType.MESH


def each_peer(me, n, body):
    if n <= 16 and n & (n - 1) == 0:
        for step in range(n - 1, 0, -1):
            peer = me
            for bit in (1, 2, 4, 8):
                if step & bit:
                    peer = peer + bit - 2 * bit * lax.rem(me // bit, 2)
            body(peer)
    else:

        @pl.loop(1, n)
        def _(step):
            body(lax.rem(me + step, n))


def kernel(
    n, values, rows_in, cols_in, live_in, bias_in, plain, relative, numerator,
    tiles, rows, cols, live, bias, scales0, scales1, send0, send1, recv0, recv1,
    tile_sem, small_sem, out_sem, in_sem,
):
    group = lax.axis_index("groups")
    me = lax.axis_index("tile")
    slots, width = values.shape[0], values.shape[1]
    parts = width // LANES
    messages = parts + 1

    smalls = [
        pltpu.make_async_copy(source, target, small_sem.at[index])
        for index, (source, target) in enumerate(
            ((bias_in, bias), (rows_in, rows), (cols_in, cols), (live_in, live))
        )
    ]
    loads = [
        pltpu.make_async_copy(values.at[slot], tiles.at[slot], tile_sem.at[slot])
        for slot in range(slots)
    ]
    for copy in smalls + loads:
        copy.start()

    barrier = pltpu.get_barrier_semaphore()
    each_peer(
        me,
        n,
        lambda peer: pl.semaphore_signal(
            barrier, inc=1, device_id=(group, peer), device_id_type=MESH
        ),
    )

    smalls[0].wait()
    for part in range(parts):
        scales0[me, part : part + 1, :] = bias[:, part * LANES : (part + 1) * LANES]
    pl.semaphore_wait(barrier, n - 1)

    def gather_start(scales, phase):
        each_peer(
            me,
            n,
            lambda peer: pltpu.make_async_remote_copy(
                src_ref=scales.at[me, pl.ds(0, parts)],
                dst_ref=scales.at[me, pl.ds(0, parts)],
                send_sem=out_sem.at[phase],
                recv_sem=in_sem.at[phase],
                device_id=(group, peer),
                device_id_type=MESH,
            ).start(),
        )

    def reduce_start(send, recv, phase):
        each_peer(
            me,
            n,
            lambda peer: pltpu.make_async_remote_copy(
                src_ref=send.at[peer, pl.ds(0, messages)],
                dst_ref=recv.at[me, pl.ds(0, messages)],
                send_sem=out_sem.at[phase],
                recv_sem=in_sem.at[phase],
                device_id=(group, peer),
                device_id_type=MESH,
            ).start(),
        )

    def arrived(buffer, sem, count):
        every = buffer.at[pl.ds(0, n - 1), pl.ds(0, count)]
        pltpu.make_async_copy(every, every, sem).wait()

    def as_row(buffer, index):
        return jnp.concatenate(
            [buffer[index, part : part + 1, :] for part in range(parts)], axis=1
        )

    def halves(vector):
        upper = vector.astype(jnp.bfloat16).astype(jnp.float32)
        return upper, vector - upper

    place = lax.broadcasted_iota(jnp.int32, (2 * n, width), 0)
    is_upper = place < n
    owner = jnp.where(is_upper, place, place - n)
    line = lax.broadcasted_iota(jnp.int32, (16, width), 0)

    def for_owner(vector, weight, target):
        upper, lower = halves(vector * weight)
        pair = jnp.where(is_upper, upper, lower)
        return jnp.where(owner == target, pair, 0.0).astype(jnp.bfloat16)

    def as_pair(vector, weight):
        upper, lower = halves(vector * weight)
        pair = jnp.where(line == 0, upper, jnp.where(line == 1, lower, 0.0))
        return pair.astype(jnp.bfloat16)

    def times(left, slot):
        return jnp.dot(left, tiles[slot], preferred_element_type=jnp.float32)

    def times_transposed(left, slot):
        return lax.dot_general(
            left, tiles[slot], (((1,), (1,)), ((), ())), preferred_element_type=jnp.float32
        )

    held = jnp.minimum(BAND, n - me)
    grands = []
    mine = None
    for sweep, (scales, send, recv) in enumerate(
        ((scales0, send0, recv0), (scales1, send1, recv1))
    ):
        gather_start(scales, 2 * sweep)
        if sweep == 0:
            for copy in smalls[1:]:
                copy.wait()
            mine = scales[me, 0:parts, :]
        band_cols = [cols[slot] for slot in range(BAND)]
        band_weights = [
            jnp.where(band_cols[slot] == me, 0.5, 1.0)
            * jnp.where(slot < held, 1.0, 0.0)
            for slot in range(BAND)
        ]
        own_row = as_row(scales, me)
        to_cols = jnp.zeros((2 * n, width), jnp.float32)
        for slot in range(BAND):
            if sweep == 0:
                loads[slot].wait()
            to_cols += times(for_owner(own_row, band_weights[slot], band_cols[slot]), slot)
        if sweep == 0:
            for copy in loads[BAND:]:
                copy.wait()

        arrived(scales, in_sem.at[2 * sweep], parts)
        to_rows = jnp.zeros((n, width), jnp.float32)
        for extra in range(TRANS):
            slot = held + extra
            row, col = rows[slot], cols[slot]
            weight = jnp.where(row == col, 0.5, 1.0) * live[slot].astype(jnp.float32)
            to_cols += times(for_owner(as_row(scales, row), weight, col), slot)
            found = times_transposed(as_pair(as_row(scales, col), weight), slot)
            found = found[0:1] + found[1:2]
            to_rows += jnp.where(owner[:n] == row, found, 0.0)
        once = to_cols[:n] + to_cols[n:]
        both = once + to_rows
        flat_scales = scales.reshape(n * 8, LANES)
        flat_send = send.reshape(n * 8, LANES)
        form = jnp.zeros((n, LANES), jnp.float32)
        for part in range(parts):
            lanes = slice(part * LANES, (part + 1) * LANES)
            flat_send[pl.ds(part, n, stride=8), :] = both[:, lanes]
            form += once[:, lanes] * flat_scales[pl.ds(part, n, stride=8), :]
        form = jnp.sum(form, axis=0, keepdims=True)
        flat_send[pl.ds(parts, n, stride=8), :] = jnp.broadcast_to(form, (n, LANES))
        reduce_start(send, recv, 2 * sweep + 1)

        owned = jnp.zeros((16, width), jnp.float32)
        for slot in range(BAND):
            pair = as_pair(as_row(scales, band_cols[slot]), band_weights[slot])
            owned += times_transposed(pair, slot)
        owned = owned[0:1] + owned[1:2]
        owned += jnp.sum(jnp.where(owner[:n] == me, both, 0.0), axis=0, keepdims=True)
        for part in range(parts):
            recv[me, part : part + 1, :] = owned[:, part * LANES : (part + 1) * LANES]
        recv[me, parts:messages, :] = form
        arrived(recv, in_sem.at[2 * sweep + 1], messages)
        total = jnp.sum(recv[:, 0:messages, :], axis=0)
        grands.append(2.0 * jnp.sum(total[parts:messages], keepdims=True))
        total = total[0:parts]
        if sweep + 1 < ITERS:
            mine = 1.0 / total
            scales1[me, 0:parts, :] = mine

    bins = float(n * width)
    factor = total * (bins / grands[1])
    raised = mine * (grands[0] / bins)
    for part in range(parts):
        lanes = slice(part * LANES, (part + 1) * LANES)
        plain[:, lanes] = mine[part : part + 1]
        relative[:, lanes] = factor[part : part + 1]
        numerator[:, lanes] = raised[part : part + 1]
    for phase, buffer in enumerate((scales0, send0, scales1, send1)):
        arrived(buffer, out_sem.at[phase], (parts, messages)[phase % 2])


def solution(mesh):
    n = mesh.shape["tile"]

    def shards(tile_values, tile_rows, tile_cols, tile_live, bias):
        slots, width = tile_values.shape[0], tile_values.shape[1]
        block = pltpu.VMEM((n, 8, LANES), jnp.float32)
        plain, relative, numerator = pl.pallas_call(
            functools.partial(kernel, n),
            out_shape=(jax.ShapeDtypeStruct(bias.shape, jnp.float32),) * 3,
            in_specs=[pl.BlockSpec(memory_space=pl.ANY)] * 5,
            out_specs=(pl.BlockSpec(memory_space=pltpu.VMEM),) * 3,
            scratch_shapes=[
                pltpu.VMEM((slots, width, width), jnp.bfloat16),
                pltpu.SMEM((slots,), jnp.int32),
                pltpu.SMEM((slots,), jnp.int32),
                pltpu.SMEM((slots,), jnp.int32),
                pltpu.VMEM(bias.shape, jnp.float32),
                block, block, block, block, block, block,
                pltpu.SemaphoreType.DMA((slots,)),
                pltpu.SemaphoreType.DMA((4,)),
                pltpu.SemaphoreType.DMA((4,)),
                pltpu.SemaphoreType.DMA((4,)),
            ],
            compiler_params=pltpu.CompilerParams(
                collective_id=0, has_side_effects=True, vmem_limit_bytes=64 * 1024 * 1024 - 65536
            ),
        )(tile_values, tile_rows, tile_cols, tile_live, bias)
        coverage = plain * relative
        return numerator / coverage, coverage

    placed = (
        P(("groups", "tile"), None, None),
        P(("groups", "tile")),
        P(("groups", "tile")),
        P(("groups", "tile")),
        P(("groups", "tile"), None),
    )
    return jax.shard_map(
        shards,
        mesh=mesh,
        in_specs=placed,
        out_specs=(P(("groups", "tile"), None), P(("groups", "tile"), None)),
        check_vma=False,
    )
```

```python
import functools

import jax
import jax.numpy as jnp
from jax import lax
from jax.experimental import pallas as pl
from jax.experimental.pallas import tpu as pltpu
from jax.sharding import PartitionSpec as P

ITERS = 2
BAND = 8
TRANS = 2
LANES = 128
MESH = pl.DeviceIdType.MESH


def each_peer(me, n, body):
    if n <= 16 and n & (n - 1) == 0:
        for step in range(n - 1, 0, -1):
            peer = me
            for bit in (1, 2, 4, 8):
                if step & bit:
                    peer = peer + bit - 2 * bit * lax.rem(me // bit, 2)
            body(peer)
    else:

        @pl.loop(1, n)
        def _(step):
            body(lax.rem(me + step, n))


def kernel(
    n, values, rows_in, cols_in, live_in, bias_in, plain, relative, numerator,
    tiles, rows, cols, live, bias, scales0, scales1, send0, send1, recv0, recv1,
    tile_sem, small_sem, out_sem, in_sem,
):
    group = lax.axis_index("groups")
    me = lax.axis_index("tile")
    slots, width = values.shape[0], values.shape[1]
    parts = width // LANES
    messages = parts + 1

    smalls = [
        pltpu.make_async_copy(source, target, small_sem.at[index])
        for index, (source, target) in enumerate(
            ((bias_in, bias), (rows_in, rows), (cols_in, cols), (live_in, live))
        )
    ]
    loads = [
        pltpu.make_async_copy(values.at[slot], tiles.at[slot], tile_sem.at[slot])
        for slot in range(slots)
    ]
    for copy in smalls + loads:
        copy.start()

    barrier = pltpu.get_barrier_semaphore()
    each_peer(
        me,
        n,
        lambda peer: pl.semaphore_signal(
            barrier, inc=1, device_id=(group, peer), device_id_type=MESH
        ),
    )

    smalls[0].wait()
    for part in range(parts):
        scales0[me, part : part + 1, :] = bias[:, part * LANES : (part + 1) * LANES]

    def gather_start(scales, phase):
        each_peer(
            me,
            n,
            lambda peer: pltpu.make_async_remote_copy(
                src_ref=scales.at[me, pl.ds(0, parts)],
                dst_ref=scales.at[me, pl.ds(0, parts)],
                send_sem=out_sem.at[phase],
                recv_sem=in_sem.at[phase],
                device_id=(group, peer),
                device_id_type=MESH,
            ).start(),
        )

    def reduce_start(send, recv, phase):
        each_peer(
            me,
            n,
            lambda peer: pltpu.make_async_remote_copy(
                src_ref=send.at[peer, pl.ds(0, messages)],
                dst_ref=recv.at[me, pl.ds(0, messages)],
                send_sem=out_sem.at[phase],
                recv_sem=in_sem.at[phase],
                device_id=(group, peer),
                device_id_type=MESH,
            ).start(),
        )

    def arrived(buffer, sem, count):
        every = buffer.at[pl.ds(0, n - 1), pl.ds(0, count)]
        pltpu.make_async_copy(every, every, sem).wait()

    def as_row(buffer, index):
        return jnp.concatenate(
            [buffer[index, part : part + 1, :] for part in range(parts)], axis=1
        )

    def halves(vector):
        upper = vector.astype(jnp.bfloat16).astype(jnp.float32)
        return upper, vector - upper

    place = lax.broadcasted_iota(jnp.int32, (2 * n, width), 0)
    is_upper = place < n
    owner = jnp.where(is_upper, place, place - n)
    line = lax.broadcasted_iota(jnp.int32, (16, width), 0)

    def for_owner(vector, weight, target):
        upper, lower = halves(vector * weight)
        pair = jnp.where(is_upper, upper, lower)
        return jnp.where(owner == target, pair, 0.0).astype(jnp.bfloat16)

    def as_pair(vector, weight):
        upper, lower = halves(vector * weight)
        pair = jnp.where(line == 0, upper, jnp.where(line == 1, lower, 0.0))
        return pair.astype(jnp.bfloat16)

    def times(left, slot):
        return jnp.dot(left, tiles[slot], preferred_element_type=jnp.float32)

    def times_transposed(left, slot):
        return lax.dot_general(
            left, tiles[slot], (((1,), (1,)), ((), ())), preferred_element_type=jnp.float32
        )

    held = jnp.minimum(BAND, n - me)
    grands = []
    mine = None
    for sweep, (scales, send, recv) in enumerate(
        ((scales0, send0, recv0), (scales1, send1, recv1))
    ):
        if sweep > 0:
            gather_start(scales, 2 * sweep)
        else:
            for copy in smalls[1:]:
                copy.wait()
            mine = scales[me, 0:parts, :]
        band_cols = [cols[slot] for slot in range(BAND)]
        band_weights = [
            jnp.where(band_cols[slot] == me, 0.5, 1.0)
            * jnp.where(slot < held, 1.0, 0.0)
            for slot in range(BAND)
        ]
        own_row = as_row(scales, me)
        to_cols = jnp.zeros((2 * n, width), jnp.float32)
        for slot in range(BAND):
            if sweep == 0:
                loads[slot].wait()
            to_cols += times(for_owner(own_row, band_weights[slot], band_cols[slot]), slot)
        if sweep == 0:
            for copy in loads[BAND:]:
                copy.wait()
            pl.semaphore_wait(barrier, n - 1)
            gather_start(scales, 0)

        arrived(scales, in_sem.at[2 * sweep], parts)
        to_rows = jnp.zeros((n, width), jnp.float32)
        for extra in range(TRANS):
            slot = held + extra
            row, col = rows[slot], cols[slot]
            weight = jnp.where(row == col, 0.5, 1.0) * live[slot].astype(jnp.float32)
            to_cols += times(for_owner(as_row(scales, row), weight, col), slot)
            found = times_transposed(as_pair(as_row(scales, col), weight), slot)
            found = found[0:1] + found[1:2]
            to_rows += jnp.where(owner[:n] == row, found, 0.0)
        once = to_cols[:n] + to_cols[n:]
        both = once + to_rows
        flat_scales = scales.reshape(n * 8, LANES)
        flat_send = send.reshape(n * 8, LANES)
        form = jnp.zeros((n, LANES), jnp.float32)
        for part in range(parts):
            lanes = slice(part * LANES, (part + 1) * LANES)
            flat_send[pl.ds(part, n, stride=8), :] = both[:, lanes]
            form += once[:, lanes] * flat_scales[pl.ds(part, n, stride=8), :]
        form = jnp.sum(form, axis=0, keepdims=True)
        flat_send[pl.ds(parts, n, stride=8), :] = jnp.broadcast_to(form, (n, LANES))
        reduce_start(send, recv, 2 * sweep + 1)

        owned = jnp.zeros((16, width), jnp.float32)
        for slot in range(BAND):
            pair = as_pair(as_row(scales, band_cols[slot]), band_weights[slot])
            owned += times_transposed(pair, slot)
        owned = owned[0:1] + owned[1:2]
        owned += jnp.sum(jnp.where(owner[:n] == me, both, 0.0), axis=0, keepdims=True)
        for part in range(parts):
            recv[me, part : part + 1, :] = owned[:, part * LANES : (part + 1) * LANES]
        recv[me, parts:messages, :] = form
        arrived(recv, in_sem.at[2 * sweep + 1], messages)
        total = jnp.sum(recv[:, 0:messages, :], axis=0)
        grands.append(2.0 * jnp.sum(total[parts:messages], keepdims=True))
        total = total[0:parts]
        if sweep + 1 < ITERS:
            mine = 1.0 / total
            scales1[me, 0:parts, :] = mine

    bins = float(n * width)
    factor = total * (bins / grands[1])
    raised = mine * (grands[0] / bins)
    for part in range(parts):
        lanes = slice(part * LANES, (part + 1) * LANES)
        plain[:, lanes] = mine[part : part + 1]
        relative[:, lanes] = factor[part : part + 1]
        numerator[:, lanes] = raised[part : part + 1]
    for phase, buffer in enumerate((scales0, send0, scales1, send1)):
        arrived(buffer, out_sem.at[phase], (parts, messages)[phase % 2])


def solution(mesh):
    n = mesh.shape["tile"]

    def shards(tile_values, tile_rows, tile_cols, tile_live, bias):
        slots, width = tile_values.shape[0], tile_values.shape[1]
        block = pltpu.VMEM((n, 8, LANES), jnp.float32)
        plain, relative, numerator = pl.pallas_call(
            functools.partial(kernel, n),
            out_shape=(jax.ShapeDtypeStruct(bias.shape, jnp.float32),) * 3,
            in_specs=[pl.BlockSpec(memory_space=pl.ANY)] * 5,
            out_specs=(pl.BlockSpec(memory_space=pltpu.VMEM),) * 3,
            scratch_shapes=[
                pltpu.VMEM((slots, width, width), jnp.bfloat16),
                pltpu.SMEM((slots,), jnp.int32),
                pltpu.SMEM((slots,), jnp.int32),
                pltpu.SMEM((slots,), jnp.int32),
                pltpu.VMEM(bias.shape, jnp.float32),
                block, block, block, block, block, block,
                pltpu.SemaphoreType.DMA((slots,)),
                pltpu.SemaphoreType.DMA((4,)),
                pltpu.SemaphoreType.DMA((4,)),
                pltpu.SemaphoreType.DMA((4,)),
            ],
            compiler_params=pltpu.CompilerParams(
                collective_id=0, has_side_effects=True, vmem_limit_bytes=64 * 1024 * 1024 - 65536
            ),
        )(tile_values, tile_rows, tile_cols, tile_live, bias)
        coverage = plain * relative
        return numerator / coverage, coverage

    placed = (
        P(("groups", "tile"), None, None),
        P(("groups", "tile")),
        P(("groups", "tile")),
        P(("groups", "tile")),
        P(("groups", "tile"), None),
    )
    return jax.shard_map(
        shards,
        mesh=mesh,
        in_specs=placed,
        out_specs=(P(("groups", "tile"), None), P(("groups", "tile"), None)),
        check_vma=False,
    )
```
